256 devices in a mesh: dp: 16 (over x, y_hi, core), tensor: 16 (over z, y_lo).
Axes of the slice: x: 4, y: 4 (y_hi: 2, y_lo: 2; y = y_hi * 2 + y_lo), z: 8, core: 2. Of those that a mesh axis runs over, the one named last changes fastest.
Arguments:
- tokens: bfloat16 [8192, 4096], P(('dp', 'tensor')), may hold values from -120 to 120
- norm_gain: float32 [4096], replicated, may hold values from 0.5 to 1.5
- w_gate: bfloat16 [4096, 8192], P('dp', 'tensor'), may hold values from -0.09375 to 0.09375
- w_up: bfloat16 [4096, 8192], P('dp', 'tensor'), may hold values from -0.09375 to 0.09375
- probes: bfloat16 [4096, 2, 8192], P('dp', None, 'tensor'), may hold values from -0.09375 to 0.09375
- cotangent: bfloat16 [8192, 8192], P('dp', 'tensor'), may hold values from -6 to 6
Outputs:
- hvp: float32 [4096, 2, 8192], P('dp', None, 'tensor')
The draws below stay inside these ranges and needn't reach their ends.
All inputs are finite; a program needn't handle non-finite values.
Results may differ from the reference program's by a relative error of at most 0.014.
Values may be sent and summed in bfloat16 or wider, within the bound.
No kernel may reach another device: no remote copies, remote signals or barrier semaphores. Data moves between devices by JAX's collectives and lax.ppermute only.
A program may use at most 64 MiB of HBM per device.

```python
import math
import jax
import jax.numpy as jnp
from jax import lax

D = 4096
FF = 8192
PROBES = 2
TOK_GROUP = 512
TOKENS = 8192
N_DP = 16


def draw_tokens(key, part):
    key_rows, key_cols, key_base = jax.random.split(key, 3)
    row_scale = jnp.exp(jax.random.uniform(key_rows, (TOKENS, 1), jnp.float32, 0.0, math.log(10.0)))
    col_scale = jnp.exp(jax.random.uniform(key_cols, (1, D), jnp.float32, 0.0, math.log(10.0)))
    base = jax.random.normal(key_base, (TOKENS, D), jnp.float32)
    base = jnp.clip(base, -4.0, 4.0)
    return (base * row_scale * col_scale * 0.3).astype(jnp.bfloat16)


def shard_levels(key, extent, pieces, smallest, top_value):
    loudness = 1.0
    for dim, shards_of in pieces:
        draws = jax.random.uniform(jax.random.fold_in(jax.random.fold_in(key, 6), dim), (shards_of,), jnp.float32, smallest / len(pieces), top_value / len(pieces))
        loudness = loudness * jnp.repeat(jnp.exp(draws), extent[dim] // shards_of).reshape((-1,) + (1,) * (len(extent) - 1 - dim))
    return loudness


def gaussian(stream_key, shape, spread, most, cuts=(), dtype=jnp.bfloat16):
    factor_of = shard_levels(stream_key, shape, cuts, -0.22, 0.18) if cuts else 1.0
    entries = jax.random.normal(stream_key, shape, jnp.float32) * spread * factor_of
    return jnp.minimum(jnp.maximum(entries, -most), most).astype(dtype)


def setup_inputs(seed: int = 0) -> dict:
    splits = jax.random.split(jax.random.key(seed), 7)
    return {
        "tokens": draw_tokens(jax.random.fold_in(splits[6], 71), 0),
        "norm_gain": jnp.clip(1.0 + 0.1 * jax.random.normal(splits[1], (D,), jnp.float32), 0.5, 1.5),
        "w_gate": gaussian(splits[2], (D, FF), D ** -0.5, 0.09375, ((0, 16), (1, 16))),
        "w_up": gaussian(splits[3], (D, FF), D ** -0.5, 0.09375, ((0, 16), (1, 16))),
        "probes": gaussian(splits[4], (D, PROBES, FF), D ** -0.5, 0.09375, ((0, 16), (2, 16))),
        "cotangent": gaussian(splits[5], (TOKENS, FF), 1.0, 6.0, ((0, 16), (1, 16))),
    }


def reference(tokens, norm_gain, w_gate, w_up, probes, cotangent):
    values = tokens.astype(jnp.float32)
    inverse = lax.rsqrt(lax.optimization_barrier(jnp.mean(values * values, axis=1, keepdims=True)) + 1e-05)
    normed = (values * inverse * norm_gain).astype(jnp.bfloat16)
    gate_pre = jnp.dot(normed, w_gate, preferred_element_type=jnp.float32)
    up_pre = jnp.dot(normed, w_up, preferred_element_type=jnp.float32)
    model_depth, probe_count, unit_count = probes.shape
    tangent = jnp.dot(normed, probes.reshape(model_depth, probe_count * unit_count), preferred_element_type=jnp.float32)
    tangent = tangent.reshape(normed.shape[0], probe_count, unit_count)
    logistic = jax.nn.sigmoid(gate_pre)
    curve = logistic * (1.0 - logistic) * (2.0 + gate_pre * (1.0 - 2.0 * logistic))
    weighting = cotangent.astype(jnp.float32) * curve * up_pre * (1.0 / math.sqrt(TOKENS))
    second = (weighting[:, None, :] * tangent).astype(jnp.bfloat16)
    grouped_rows = normed.reshape(N_DP, TOK_GROUP, model_depth)
    grouped_terms = second.reshape(N_DP, TOK_GROUP, probe_count * unit_count)

    def accumulate(totals, group_pair):
        partial_sum = jnp.dot(group_pair[0].T, group_pair[1], preferred_element_type=jnp.float32)
        rounded = lax.optimization_barrier(partial_sum.astype(jnp.bfloat16))
        return (totals + rounded.astype(jnp.float32), None)
    start_totals = jnp.zeros((model_depth, probe_count * unit_count), jnp.float32)
    totals, unused = lax.scan(accumulate, start_totals, (grouped_rows, grouped_terms))
    return totals.reshape(model_depth, probe_count, unit_count)
```

```python
import math

import jax
import jax.numpy as jnp
from jax import lax
from jax.experimental import pallas as pl
from jax.experimental.pallas import tpu as pltpu
from jax.sharding import Mesh, PartitionSpec as P

NX, NYH, NC, NZ, NYL = 4, 2, 2, 8, 2
AXES = ("x", "yh", "c", "z", "yl")
VMEM_BYTES = 58 * 1024 * 1024


def ring_perm(spots, step):
    size = len(spots[0])
    return [
        (line[i], line[(i + sign * step) % size])
        for line, sign in zip(spots, (1, -1))
        for i in range(size)
    ]


def along_x(v, step):
    return lax.ppermute(
        v, ("x", "c"), ring_perm([[x * 2 + c for x in range(NX)] for c in range(NC)], step)
    )


def along_y(v, step):
    spots = [[(yh * 2 + c) * 2 + yl for yh in range(NYH) for yl in range(NYL)] for c in range(NC)]
    return lax.ppermute(v, ("yh", "c", "yl"), ring_perm(spots, step))


def along_z(v, step):
    return lax.ppermute(
        v, ("c", "z"), ring_perm([[c * NZ + z for z in range(NZ)] for c in range(NC)], step)
    )


def swap_core(v):
    return lax.ppermute(v, "c", [(0, 1), (1, 0)])


def swap_yh(v):
    return lax.ppermute(v, "yh", [(0, 1), (1, 0)])


def norm_kernel(pos, tokens, gain, out_a, out_b):
    x, c = pos[0], pos[2]
    rows, depth = tokens.shape
    piece = depth // 16
    values = tokens[...].astype(jnp.float32)
    inverse = lax.rsqrt(jnp.mean(values * values, axis=1, keepdims=True) + 1e-05)
    for r in range(NX):
        xs = lax.rem(x + jnp.where(c == 0, NX - r, r), NX)
        for yh in range(NYH):
            for crel in range(NC):
                cs = jnp.where(crel == 0, c, 1 - c)
                source = pl.multiple_of((xs * 4 + yh * 2 + cs) * piece, piece)
                block = tokens[:, pl.ds(source, piece)].astype(jnp.float32)
                normed = (block * inverse * gain[:, pl.ds(source, piece)]).astype(jnp.bfloat16)
                b = r * 4 + yh * 2 + crel
                out_a[:, b * piece : (b + 1) * piece] = normed[: rows // 2]
                out_b[:, b * piece : (b + 1) * piece] = normed[rows // 2 :]


def normalize(pos, tokens, gain):
    rows, depth = tokens.shape
    half = jax.ShapeDtypeStruct((rows // 2, depth), jnp.bfloat16)
    return pl.pallas_call(
        norm_kernel,
        out_shape=(half, half),
        in_specs=[
            pl.BlockSpec(memory_space=pltpu.SMEM),
            pl.BlockSpec(memory_space=pltpu.VMEM),
            pl.BlockSpec(memory_space=pltpu.VMEM),
        ],
        out_specs=(pl.BlockSpec(memory_space=pltpu.VMEM),) * 2,
        compiler_params=pltpu.CompilerParams(vmem_limit_bytes=VMEM_BYTES),
        name="rms_norm",
    )(pos, tokens, gain.reshape(1, depth))


def main_kernel(scale, pos, *refs):
    na = refs[0:8]
    nb = refs[8:12]
    keep = refs[12:16]
    recv = refs[16:20]
    skeep = refs[20:24]
    srecv = refs[24:28]
    cot_keep, cot_recv = refs[28:30]
    out_own, out_sib = refs[30:32]
    nsc, wsc, csc, ssc, nsem, wsem, csem = refs[32:]
    yh, c, z, yl = pos[1], pos[2], pos[3], pos[4]
    y = yh * 2 + yl
    copies = []

    def copy(src, dst, sem):
        op = pltpu.make_async_copy(src, dst, sem)
        op.start()
        copies.append(op)

    units = wsc.shape[1] // 4
    for k in range(NX):
        for mine, bunch, crel in (
            (True, keep, 0), (False, recv, 0), (True, skeep, 1), (False, srecv, 1),
        ):
            r = k if crel == 0 else (NX - k) % NX
            row = (r * 4 + crel) * 256 + jnp.where(mine, yh, 1 - yh) * 512
            copy(bunch[k], wsc.at[pl.ds(pl.multiple_of(row, 256), 256)], wsem.at[len(copies)])
    n_w = len(copies)
    group = cot_keep.shape[0]
    copy(cot_keep, csc.at[pl.ds(pl.multiple_of(yh * group, group), group)], csem.at[0])
    copy(cot_recv, csc.at[pl.ds(pl.multiple_of((1 - yh) * group, group), group)], csem.at[1])

    def token_row(yi, zi, half):
        row = (yi // 2) * group + (zi * 2 + lax.rem(yi, 2)) * 32 + half * 16
        return pl.multiple_of(row, 16)

    n_n = 0
    for k in range(NZ):
        zi = lax.rem(z + jnp.where(c == 0, NZ - k, k), NZ)
        for i in range(4):
            yi = lax.rem(y + jnp.where(c == 0, 4 - i, i), 4)
            copy(na[k].at[pl.ds(i * 16, 16)], nsc.at[pl.ds(token_row(yi, zi, 0), 16)], nsem.at[n_n])
            n_n += 1
    for i in range(4):
        yi = lax.rem(y + jnp.where(c == 0, 4 - i, i), 4)
        for k in range(NZ):
            zi = lax.rem(z + jnp.where(c == 0, NZ - k, k), NZ)
            copy(nb[i].at[pl.ds(k * 16, 16)], nsc.at[pl.ds(token_row(yi, zi, 1), 16)], nsem.at[n_n])
            n_n += 1
    for op in copies:
        op.wait()

    def project(t, carry):
        rows = pl.ds(pl.multiple_of(t * 256, 256), 256)
        block = nsc[rows, :]

        def mul(j):
            return jnp.dot(
                block, wsc[:, j * units : (j + 1) * units], preferred_element_type=jnp.float32
            )

        gate = mul(0)
        logistic = jax.nn.sigmoid(gate)
        curve = logistic * (1.0 - logistic) * (2.0 + gate * (1.0 - 2.0 * logistic))
        weighting = csc[rows, :].astype(jnp.float32) * curve * mul(1) * scale
        ssc[rows, 0:units] = (weighting * mul(2)).astype(jnp.bfloat16)
        ssc[rows, units : 2 * units] = (weighting * mul(3)).astype(jnp.bfloat16)
        return carry

    lax.fori_loop(0, nsc.shape[0] // 256, project, 0)

    def reduce(i, carry):
        for crel, out in ((0, out_own), (1, out_sib)):
            cols = pl.ds(pl.multiple_of((i * 2 + crel) * 256, 256), 256)
            out[i] = lax.dot_general(
                nsc[:, cols], ssc[...], (((0,), (0,)), ((), ())), preferred_element_type=jnp.float32
            ).astype(jnp.bfloat16)
        return carry

    lax.fori_loop(0, 8, reduce, 0)


def products(pos, na, nb, keep, recv, skeep, srecv, cot_keep, cot_recv, scale):
    depth = na[0].shape[1]
    tokens = 2 * cot_keep.shape[0]
    units = cot_keep.shape[1]
    operands = (*na, *nb, *keep, *recv, *skeep, *srecv, cot_keep, cot_recv)
    half = jax.ShapeDtypeStruct((8, 256, 2 * units), jnp.bfloat16)
    return pl.pallas_call(
        lambda *refs: main_kernel(scale, *refs),
        out_shape=(half, half),
        in_specs=[pl.BlockSpec(memory_space=pltpu.SMEM)]
        + [pl.BlockSpec(memory_space=pl.ANY)] * len(operands),
        out_specs=(pl.BlockSpec(memory_space=pltpu.VMEM),) * 2,
        scratch_shapes=[
            pltpu.VMEM((tokens, depth), jnp.bfloat16),
            pltpu.VMEM((depth, 4 * units), jnp.bfloat16),
            pltpu.VMEM((tokens, units), jnp.bfloat16),
            pltpu.VMEM((tokens, 2 * units), jnp.bfloat16),
            pltpu.SemaphoreType.DMA((64,)),
            pltpu.SemaphoreType.DMA((16,)),
            pltpu.SemaphoreType.DMA((2,)),
        ],
        compiler_params=pltpu.CompilerParams(vmem_limit_bytes=VMEM_BYTES),
        cost_estimate=pl.CostEstimate(
            flops=2 * tokens * depth * 6 * units, bytes_accessed=2**24, transcendentals=0
        ),
        name="products",
    )(pos, *operands)


def per_device(tokens, norm_gain, w_gate, w_up, probes, cotangent):
    pos = jnp.stack([lax.axis_index(a) for a in AXES]).astype(jnp.int32)
    yh = lax.axis_index("yh")
    units = w_gate.shape[1] // 2
    p0, p1 = probes[:, 0, :], probes[:, 1, :]

    def half_of(which):
        return jnp.concatenate(
            [lax.dynamic_slice_in_dim(a, which * units, units, 1) for a in (w_gate, w_up, p0, p1)],
            axis=1,
        )

    w_keep, w_send = half_of(yh), half_of(1 - yh)
    cot_keep = lax.dynamic_slice_in_dim(cotangent, yh * units, units, 1)
    cot_send = lax.dynamic_slice_in_dim(cotangent, (1 - yh) * units, units, 1)
    rows_a, rows_b = normalize(pos, tokens, norm_gain)

    w_recv = swap_yh(w_send)
    cot_recv = swap_yh(cot_send)
    first = jnp.concatenate([rows_a] + [along_y(rows_a, i) for i in (1, 2, 3)], axis=0)
    na = [first]
    for _ in range(NZ - 1):
        na.append(along_z(na[-1], 1))
    column = [rows_b]
    for _ in range(NZ - 1):
        column.append(along_z(column[-1], 1))
    nb = [jnp.concatenate(column, axis=0)]
    for _ in range(3):
        nb.append(along_y(nb[-1], 1))
    keep, recv = [w_keep], [w_recv]
    for _ in range(NX - 1):
        keep.append(along_x(keep[-1], 1))
        recv.append(along_x(recv[-1], 1))
    skeep = [swap_core(w) for w in keep]
    srecv = [swap_core(w) for w in recv]

    scale = 1.0 / math.sqrt(cotangent.shape[0] * NX * NYH * NC)
    own, sib = products(pos, na, nb, keep, recv, skeep, srecv, cot_keep, cot_recv, scale)
    own = own.reshape(NX, NYH, 256, 2 * units)
    sib = sib.reshape(NX, NYH, 256, 2 * units)
    total = None
    for r in (2, 1, 3, 0):
        other = swap_core(sib[(NX - r) % NX])
        both = own[r].astype(jnp.float32) + other.astype(jnp.float32)
        if r:
            both = along_x(both.astype(jnp.bfloat16), NX - r).astype(jnp.float32)
        total = both if total is None else total + both
    mine = lax.dynamic_index_in_dim(total, yh, 0, keepdims=False)
    theirs = lax.dynamic_index_in_dim(total, 1 - yh, 0, keepdims=False).astype(jnp.bfloat16)
    got = swap_yh(theirs).astype(jnp.float32)
    mine = mine.reshape(256, 2, units)
    got = got.reshape(256, 2, units)
    low = jnp.where(yh == 0, mine, got)
    high = jnp.where(yh == 0, got, mine)
    return jnp.concatenate([low, high], axis=2)


def solution(mesh):
    inner = Mesh(mesh.devices.reshape(NX, NYH, NC, NZ, NYL), AXES)
    dp, tensor = ("x", "yh", "c"), ("z", "yl")
    in_specs = (
        P(dp + tensor, None),
        P(),
        P(dp, tensor),
        P(dp, tensor),
        P(dp, None, tensor),
        P(dp, tensor),
    )
    return jax.shard_map(
        per_device, mesh=inner, in_specs=in_specs, out_specs=P(dp, None, tensor), check_vma=False
    )
```

```python
import math

import jax
import jax.numpy as jnp
from jax import lax
from jax.experimental import pallas as pl
from jax.experimental.pallas import tpu as pltpu
from jax.sharding import Mesh, PartitionSpec as P

NX, NYH, NC, NZ, NYL = 4, 2, 2, 8, 2
AXES = ("x", "yh", "c", "z", "yl")
VMEM_BYTES = 58 * 1024 * 1024


def ring_perm(spots, step):
    size = len(spots[0])
    return [
        (line[i], line[(i + sign * step) % size])
        for line, sign in zip(spots, (1, -1))
        for i in range(size)
    ]


def along_x(v, step):
    return lax.ppermute(
        v, ("x", "c"), ring_perm([[x * 2 + c for x in range(NX)] for c in range(NC)], step)
    )


def along_y(v, step):
    spots = [[(yh * 2 + c) * 2 + yl for yh in range(NYH) for yl in range(NYL)] for c in range(NC)]
    return lax.ppermute(v, ("yh", "c", "yl"), ring_perm(spots, step))


def swap_core(v):
    return lax.ppermute(v, "c", [(0, 1), (1, 0)])


def swap_yh(v):
    return lax.ppermute(v, "yh", [(0, 1), (1, 0)])


def norm_kernel(tokens, gain, out_a, out_b):
    x, c = lax.axis_index("x"), lax.axis_index("c")
    rows, depth = tokens.shape
    piece = depth // 16
    values = tokens[...].astype(jnp.float32)
    inverse = lax.rsqrt(jnp.mean(values * values, axis=1, keepdims=True) + 1e-05)
    for r in range(NX):
        xs = lax.rem(x + jnp.where(c == 0, NX - r, r), NX)
        for yh in range(NYH):
            for crel in range(NC):
                cs = jnp.where(crel == 0, c, 1 - c)
                source = pl.multiple_of((xs * 4 + yh * 2 + cs) * piece, piece)
                block = tokens[:, pl.ds(source, piece)].astype(jnp.float32)
                normed = (block * inverse * gain[:, pl.ds(source, piece)]).astype(jnp.bfloat16)
                b = r * 4 + crel * 2 + yh
                out_a[:, b * piece : (b + 1) * piece] = normed[: rows // 2]
                out_b[:, b * piece : (b + 1) * piece] = normed[rows // 2 :]


def normalize(tokens, gain):
    rows, depth = tokens.shape
    half = jax.ShapeDtypeStruct((rows // 2, depth), jnp.bfloat16)
    return pl.pallas_call(
        norm_kernel,
        out_shape=(half, half),
        in_specs=[
            pl.BlockSpec(memory_space=pltpu.VMEM),
            pl.BlockSpec(memory_space=pltpu.VMEM),
        ],
        out_specs=(pl.BlockSpec(memory_space=pltpu.VMEM),) * 2,
        compiler_params=pltpu.CompilerParams(vmem_limit_bytes=VMEM_BYTES),
        name="rms_norm",
    )(tokens, gain.reshape(1, depth))


def _a(dz):
    return [(i, dz, 0) for i in range(4)]


EARLY = (
    _a(0),
    _a(-1) + [(0, -2, 1)],
    _a(1) + [(0, 2, 1)],
    _a(-2) + [(0, -3, 1)],
    _a(2) + [(0, 3, 1)],
    _a(-3) + [(0, 4, 1)],
    _a(3),
    [(0, 0, 1)],
    [(0, -1, 1)],
    [(0, 1, 1)],
    [(2, 0, 1), (2, -1, 1), (2, 1, 1), (1, -2, 1), (1, 2, 1)],
    [(3, 0, 1), (3, -1, 1), (3, 1, 1), (2, -2, 1), (2, 2, 1), (1, -3, 1), (1, 3, 1)],
)
LATE = (
    [(1, 0, 1), (1, -1, 1), (1, 1, 1)],
    [(3, -2, 1), (3, 2, 1), (2, -3, 1), (2, 3, 1), (1, 4, 1)],
    [(3, -3, 1), (3, 3, 1), (3, 4, 1)],
    [(2, 4, 1)],
    _a(4),
)
BLOCK = 256


def rows_of(layout):
    return [16 * len(pieces) for pieces in layout]


def second_kernel(scale, layout, *refs):
    count = len(layout)
    arrays = refs[:count]
    keep, recv, cot_keep, cot_recv, out, nsc, wsc, cabs, csc, nsem, wsem, csem = refs[count:]
    x, yh, c, z, yl = (lax.axis_index(a) for a in AXES)
    y = yh * 2 + yl
    group, units = cot_keep.shape

    def copy(src, dst, sem):
        op = pltpu.make_async_copy(src, dst, sem)
        op.start()
        return op

    wait_c = [
        copy(cot_keep, cabs.at[pl.ds(pl.multiple_of(yh * group, group), group)], csem.at[0]),
        copy(cot_recv, cabs.at[pl.ds(pl.multiple_of((1 - yh) * group, group), group)], csem.at[1]),
    ]
    wait_w = []
    for xs in range(NX):
        r = lax.rem(jnp.where(c == 0, x - xs, xs - x) + NX, NX)
        for cs in range(NC):
            crel = jnp.where(c == cs, 0, 1)
            for mine, bunch in ((True, keep), (False, recv)):
                row = (r * 4 + crel * 2) * 256 + jnp.where(mine, yh, 1 - yh) * 256
                wait_w.append(
                    copy(
                        bunch.at[xs * 2 + cs],
                        wsc.at[pl.ds(pl.multiple_of(row, 256), 256)],
                        wsem.at[len(wait_w)],
                    )
                )
    wait_n, start = [], 0
    for i, (array, rows) in enumerate(zip(arrays, rows_of(layout))):
        op = copy(array.at[pl.ds(0, rows)], nsc.at[pl.ds(start, rows)], nsem.at[i])
        wait_n.append((start, op))
        start += rows
    for op in wait_c:
        op.wait()
    place = 0
    for pieces in layout:
        for dy, dz, half in pieces:
            ys = lax.rem(y + jnp.where(c == 0, 4 - dy, dy), 4)
            zs = lax.rem(z + dz + NZ, NZ)
            row = (ys // 2) * group + (zs * 2 + lax.rem(ys, 2)) * 32 + half * 16
            csc[place : place + 16, :] = cabs[pl.ds(pl.multiple_of(row, 16), 16), :]
            place += 16
    for op in wait_w:
        op.wait()
    for t in range(nsc.shape[0] // BLOCK):
        while wait_n and wait_n[0][0] < (t + 1) * BLOCK:
            wait_n.pop(0)[1].wait()
        block = nsc[t * BLOCK : (t + 1) * BLOCK, :]

        def mul(j):
            return jnp.dot(
                block, wsc[:, j * units : (j + 1) * units], preferred_element_type=jnp.float32
            )

        gate = mul(0)
        logistic = jax.nn.sigmoid(gate)
        curve = logistic * (1.0 - logistic) * (2.0 + gate * (1.0 - 2.0 * logistic))
        weighting = csc[t * BLOCK : (t + 1) * BLOCK, :].astype(jnp.float32) * curve * mul(1) * scale
        for p in range(2):
            second = weighting * mul(2 + p)
            out[p * units : (p + 1) * units, t * BLOCK : (t + 1) * BLOCK] = second.T.astype(
                jnp.bfloat16
            )


def second_factor(name, layout, arrays, keep, recv, cot_keep, cot_recv, scale):
    depth = arrays[0].shape[1]
    tokens = sum(rows_of(layout))
    group, units = cot_keep.shape
    operands = (*arrays, keep, recv, cot_keep, cot_recv)
    return pl.pallas_call(
        lambda *refs: second_kernel(scale, layout, *refs),
        out_shape=jax.ShapeDtypeStruct((2 * units, tokens), jnp.bfloat16),
        in_specs=[pl.BlockSpec(memory_space=pl.ANY)] * len(operands),
        out_specs=pl.BlockSpec(memory_space=pltpu.VMEM),
        scratch_shapes=[
            pltpu.VMEM((tokens, depth), jnp.bfloat16),
            pltpu.VMEM((depth, 4 * units), jnp.bfloat16),
            pltpu.VMEM((2 * group, units), jnp.bfloat16),
            pltpu.VMEM((tokens, units), jnp.bfloat16),
            pltpu.SemaphoreType.DMA((len(layout),)),
            pltpu.SemaphoreType.DMA((16,)),
            pltpu.SemaphoreType.DMA((2,)),
        ],
        compiler_params=pltpu.CompilerParams(vmem_limit_bytes=32 * 1024 * 1024),
        cost_estimate=pl.CostEstimate(
            flops=2**20, bytes_accessed=2**20, transcendentals=0
        ),
        name=name,
    )(*operands)


def partial_kernel(early_count, *refs):
    arrays, second_e, second_l, own, sib = refs[:-4], refs[-4], refs[-3], refs[-2], refs[-1]
    early = jnp.concatenate([a[...] for a in arrays[:early_count]], axis=0)
    late = jnp.concatenate([a[...] for a in arrays[early_count:]], axis=0)
    result = jnp.dot(second_e[...], early, preferred_element_type=jnp.float32)
    result = result + jnp.dot(second_l[...], late, preferred_element_type=jnp.float32)
    result = result.astype(jnp.bfloat16)
    step = pl.program_id(0)

    @pl.when(step == 0)
    def _():
        own[...] = result

    @pl.when(step == 1)
    def _():
        sib[...] = result


def partials(arrays, second_e, second_l, r):
    width = second_e.shape[0]
    rows = rows_of(EARLY + LATE)
    half = jax.ShapeDtypeStruct((width, 512), jnp.bfloat16)
    whole = pl.BlockSpec((width, 512), lambda j: (0, 0))
    return pl.pallas_call(
        lambda *refs: partial_kernel(len(EARLY), *refs),
        grid=(2,),
        out_shape=(half, half),
        in_specs=[pl.BlockSpec((n, 512), lambda j: (0, r * 2 + j)) for n in rows]
        + [pl.BlockSpec(a.shape, lambda j: (0, 0)) for a in (second_e, second_l)],
        out_specs=(whole, whole),
        compiler_params=pltpu.CompilerParams(vmem_limit_bytes=24 * 1024 * 1024),
        cost_estimate=pl.CostEstimate(
            flops=2**20, bytes_accessed=2**20, transcendentals=0
        ),
        name="partials_%d" % r,
    )(*arrays, second_e, second_l)


def final_kernel(m0, m1, m2, m3, got, out):
    units = out.shape[2] // 2
    yh = lax.axis_index("yh")
    mine = m0[...]
    for m in (m1, m2, m3):
        mine = mine + m[...].astype(jnp.float32)
    got = got[...].astype(jnp.float32)
    low, high = jnp.where(yh == 0, mine, got), jnp.where(yh == 0, got, mine)
    for p in range(2):
        rows = slice(p * units, (p + 1) * units)
        out[:, p, 0:units] = low[rows].T
        out[:, p, units : 2 * units] = high[rows].T


def finish(mine, got):
    width, rows = got.shape
    vmem = pl.BlockSpec(memory_space=pltpu.VMEM)
    return pl.pallas_call(
        final_kernel,
        out_shape=jax.ShapeDtypeStruct((rows, 2, width), jnp.float32),
        in_specs=[vmem] * 5,
        out_specs=vmem,
        compiler_params=pltpu.CompilerParams(vmem_limit_bytes=24 * 1024 * 1024),
        name="finish",
    )(*mine, got)


def lay_kernel(parts, *refs):
    outs = refs[len(refs) - len(parts) :]
    for part, out in zip(parts, outs):
        start = 0
        for i in part:
            n = refs[i].shape[0]
            out[start : start + n, :] = refs[i][...]
            start += n


def lay(name, pieces, parts):
    depth = pieces[0][0].shape[1]
    vmem = pl.BlockSpec(memory_space=pltpu.VMEM)
    return pl.pallas_call(
        lambda *refs: lay_kernel(parts, *refs),
        grid=(1,),
        out_shape=[
            jax.ShapeDtypeStruct((sum(pieces[i][2] for i in part), depth), jnp.bfloat16)
            for part in parts
        ],
        in_specs=[
            pl.BlockSpec((n, depth), lambda j, at=first // n: (at, 0)) for _, first, n in pieces
        ],
        out_specs=[
            pl.BlockSpec((sum(pieces[i][2] for i in part), depth), lambda j: (0, 0))
            for part in parts
        ],
        compiler_params=pltpu.CompilerParams(vmem_limit_bytes=24 * 1024 * 1024),
        name=name,
    )(*[a for a, _, _ in pieces])


def shift_z(v, step):
    return lax.ppermute(v, "z", [(i, (i + step) % NZ) for i in range(NZ)])


def per_device(tokens, norm_gain, w_gate, w_up, probes, cotangent):
    yh, c = lax.axis_index("yh"), lax.axis_index("c")
    units = w_gate.shape[1] // 2
    ordered = lax.optimization_barrier

    def half_of(which):
        return jnp.concatenate(
            [lax.dynamic_slice_in_dim(a, which * units, units, 1) for a in (w_gate, w_up, p0, p1)],
            axis=1,
        )

    a0, b0 = normalize(tokens, norm_gain)
    a0, b0, w_gate, w_up, probes, cotangent = ordered(
        (a0, b0, w_gate, w_up, probes, cotangent)
    )
    p0, p1 = probes[:, 0, :], probes[:, 1, :]
    w_keep, w_send = half_of(yh), half_of(1 - yh)
    cot_keep = lax.dynamic_slice_in_dim(cotangent, yh * units, units, 1)
    cot_send = lax.dynamic_slice_in_dim(cotangent, (1 - yh) * units, units, 1)
    keep = lax.all_gather(w_keep, ("x", "c"))

    ya = [along_y(a0, i) for i in (1, 2, 3)]
    bm, bp = shift_z(b0, 1), shift_z(b0, -1)
    *ya, bm, bp, w_send, b0 = ordered((*ya, bm, bp, w_send, b0))

    w_recv = swap_yh(w_send)
    up0, down0, y0 = lay(
        "lay_1",
        [(v, 0, 16) for v in (a0, *ya, bm, bp, b0)],
        ((0, 1, 2, 3, 4), (0, 1, 2, 3, 5), (6, 4, 5)),
    )
    up1, down1 = shift_z(up0, 1), shift_z(down0, -1)
    y1 = along_y(y0, 1)
    up1, down1, y1, w_recv = ordered((up1, down1, y1, w_recv))
    recv = lax.all_gather(w_recv, ("x", "c"))

    up2, down2 = shift_z(up1, 1), shift_z(down1, -1)
    (y,) = lay("lay_2", [(y1, 0, 48), (up1, 64, 16), (down1, 64, 16)], ((0, 1, 2),))
    y2 = along_y(y, 1)
    up2, down2, y2, cot_send = ordered((up2, down2, y2, cot_send))
    cot_recv = swap_yh(cot_send)

    up3, down3 = shift_z(up2, 1), shift_z(down2, -1)
    (y,) = lay("lay_3", [(y2, 0, 80), (up2, 64, 16), (down2, 64, 16)], ((0, 1, 2),))
    y3 = along_y(y, 1)
    up3, down3, y3, cot_recv, keep, recv = ordered((up3, down3, y3, cot_recv, keep, recv))

    a4 = lax.ppermute(
        jnp.where(c == 0, up3[:64], down3[:64]),
        ("c", "z"),
        ring_perm([[i * NZ + z for z in range(NZ)] for i in range(NC)], 1),
    )
    y, around, across = lay(
        "lay_4",
        [(y3, 48, 16), (y3, 64, 16), (y3, 80, 16), (y3, 96, 16)]
        + [(up3, 64, 16), (up2, 64, 16), (down2, 64, 16)],
        ((0, 1, 2, 3, 4), (5, 6, 4), (4,)),
    )
    y4, y5, y6 = along_y(y, 1), along_y(around, 3), along_y(across, 2)
    early = (up0, up1, down1, up2, down2, up3, down3, b0, bm, bp, y2, y3)
    late = (y1, y4, y5, y6, a4)

    scale = 1.0 / math.sqrt(cotangent.shape[0] * NX * NYH * NC)
    rest = (keep, recv, cot_keep, cot_recv, scale)
    second_e = second_factor("second_early", EARLY, early, *rest)
    second_l = second_factor("second_late", LATE, late, *rest)
    own, sib, first, last = {}, {}, {}, {}
    arrays = early + late

    def add_cores(r):
        other = swap_core(sib[(NX - r) % NX])
        both = own[r].astype(jnp.float32) + other.astype(jnp.float32)
        pair = [lax.dynamic_slice_in_dim(both, w * 256, 256, 1) for w in (1 - yh, yh)]
        if r:
            pair = [v.astype(jnp.bfloat16) for v in pair]
        return ordered(pair[0]), ordered(pair[1])

    own[2], sib[2] = partials(arrays, second_e, second_l, 2)
    own[3], sib[3] = partials(arrays, second_e, second_l, 3)
    first[2], last[2] = add_cores(2)
    first[2], last[2], second_l = ordered((first[2], last[2], second_l))
    own[1], sib[1] = partials(arrays, second_e, second_l, 1)
    first[1], last[1] = add_cores(1)
    first[1], second_l = ordered((first[1], second_l))
    own[0], sib[0] = partials(arrays, second_e, second_l, 0)
    first[3], last[3] = add_cores(3)
    first[0], last[0] = add_cores(0)
    last[2] = along_x(last[2], NX - 2)
    for r in (2, 1, 3):
        first[r] = along_x(first[r], NX - r)
    *arrived, last[1], last[3] = ordered((*(first[r] for r in range(NX)), last[1], last[3]))
    total = sum(v.astype(jnp.float32) for v in arrived)
    for r in (1, 3):
        last[r] = along_x(last[r], NX - r)
    got = swap_yh(total.astype(jnp.bfloat16))
    return finish([last[r] for r in range(NX)], got)


def solution(mesh):
    inner = Mesh(mesh.devices.reshape(NX, NYH, NC, NZ, NYL), AXES)
    dp, tensor = ("x", "yh", "c"), ("z", "yl")
    in_specs = (
        P(dp + tensor, None),
        P(),
        P(dp, tensor),
        P(dp, tensor),
        P(dp, None, tensor),
        P(dp, tensor),
    )
    return jax.shard_map(
        per_device, mesh=inner, in_specs=in_specs, out_specs=P(dp, None, tensor), check_vma=False
    )
```

```python
import math

import jax
import jax.numpy as jnp
from jax import lax
from jax.experimental import pallas as pl
from jax.experimental.pallas import tpu as pltpu
from jax.sharding import Mesh, PartitionSpec as P

NX, NYH, NC, NZ, NYL = 4, 2, 2, 8, 2
AXES = ("x", "yh", "c", "z", "yl")
VMEM_BYTES = 58 * 1024 * 1024


def ring_perm(spots, step):
    size = len(spots[0])
    return [
        (line[i], line[(i + sign * step) % size])
        for line, sign in zip(spots, (1, -1))
        for i in range(size)
    ]


def along_x(v, step):
    return lax.ppermute(
        v, ("x", "c"), ring_perm([[x * 2 + c for x in range(NX)] for c in range(NC)], step)
    )


def along_y(v, step):
    spots = [[(yh * 2 + c) * 2 + yl for yh in range(NYH) for yl in range(NYL)] for c in range(NC)]
    return lax.ppermute(v, ("yh", "c", "yl"), ring_perm(spots, step))


def swap_core(v):
    return lax.ppermute(v, "c", [(0, 1), (1, 0)])


def swap_yh(v):
    return lax.ppermute(v, "yh", [(0, 1), (1, 0)])


def norm_kernel(tokens, gain, out_a, out_b):
    x, c = lax.axis_index("x"), lax.axis_index("c")
    rows, depth = tokens.shape
    piece = depth // 16
    values = tokens[...].astype(jnp.float32)
    inverse = lax.rsqrt(jnp.mean(values * values, axis=1, keepdims=True) + 1e-05)
    for r in range(NX):
        xs = lax.rem(x + jnp.where(c == 0, NX - r, r), NX)
        for yh in range(NYH):
            for crel in range(NC):
                cs = jnp.where(crel == 0, c, 1 - c)
                source = pl.multiple_of((xs * 4 + yh * 2 + cs) * piece, piece)
                block = tokens[:, pl.ds(source, piece)].astype(jnp.float32)
                normed = (block * inverse * gain[:, pl.ds(source, piece)]).astype(jnp.bfloat16)
                b = r * 4 + crel * 2 + yh
                out_a[:, b * piece : (b + 1) * piece] = normed[: rows // 2]
                out_b[:, b * piece : (b + 1) * piece] = normed[rows // 2 :]


def normalize(tokens, gain):
    rows, depth = tokens.shape
    half = jax.ShapeDtypeStruct((rows // 2, depth), jnp.bfloat16)
    return pl.pallas_call(
        norm_kernel,
        out_shape=(half, half),
        in_specs=[
            pl.BlockSpec(memory_space=pltpu.VMEM),
            pl.BlockSpec(memory_space=pltpu.VMEM),
        ],
        out_specs=(pl.BlockSpec(memory_space=pltpu.VMEM),) * 2,
        compiler_params=pltpu.CompilerParams(vmem_limit_bytes=VMEM_BYTES),
        name="rms_norm",
    )(tokens, gain.reshape(1, depth))


def _a(dz):
    return [(i, dz, 0) for i in range(4)]


EARLY = (
    _a(0),
    _a(-1) + [(0, -2, 1)],
    _a(1) + [(0, 2, 1)],
    _a(-2) + [(0, -3, 1)],
    _a(2) + [(0, 3, 1)],
    _a(-3) + [(0, 4, 1)],
    _a(3),
    [(0, 0, 1)],
    [(0, -1, 1)],
    [(0, 1, 1)],
    [(2, 0, 1), (2, -1, 1), (2, 1, 1), (1, -2, 1), (1, 2, 1)],
    [(3, 0, 1), (3, -1, 1), (3, 1, 1), (2, -2, 1), (2, 2, 1), (1, -3, 1), (1, 3, 1)],
)
LATE = (
    [(1, 0, 1), (1, -1, 1), (1, 1, 1)],
    [(3, -2, 1), (3, 2, 1), (2, -3, 1), (2, 3, 1), (1, 4, 1)],
    [(3, -3, 1), (3, 3, 1), (3, 4, 1)],
    [(2, 4, 1)],
    _a(4),
)
BLOCK = 256


def rows_of(layout):
    return [16 * len(pieces) for pieces in layout]


def second_kernel(scale, layout, *refs):
    count = len(layout)
    arrays = refs[:count]
    keep, recv, cot_keep, cot_recv, out, laid = refs[count : count + 6]
    nsc, wsc, cabs, csc, nsem, wsem, csem, osem = refs[count + 6 :]
    x, yh, c, z, yl = (lax.axis_index(a) for a in AXES)
    y = yh * 2 + yl
    group, units = cot_keep.shape

    def copy(src, dst, sem):
        op = pltpu.make_async_copy(src, dst, sem)
        op.start()
        return op

    wait_c = [
        copy(cot_keep, cabs.at[pl.ds(pl.multiple_of(yh * group, group), group)], csem.at[0]),
        copy(cot_recv, cabs.at[pl.ds(pl.multiple_of((1 - yh) * group, group), group)], csem.at[1]),
    ]
    wait_w = []
    for xs in range(NX):
        r = lax.rem(jnp.where(c == 0, x - xs, xs - x) + NX, NX)
        for cs in range(NC):
            crel = jnp.where(c == cs, 0, 1)
            for mine, bunch in ((True, keep), (False, recv)):
                row = (r * 4 + crel * 2) * 256 + jnp.where(mine, yh, 1 - yh) * 256
                wait_w.append(
                    copy(
                        bunch.at[xs * 2 + cs],
                        wsc.at[pl.ds(pl.multiple_of(row, 256), 256)],
                        wsem.at[len(wait_w)],
                    )
                )
    wait_n, start = [], 0
    for i, (array, rows) in enumerate(zip(arrays, rows_of(layout))):
        op = copy(array.at[pl.ds(0, rows)], nsc.at[pl.ds(start, rows)], nsem.at[i])
        wait_n.append((start, op))
        start += rows
    for op in wait_c:
        op.wait()
    place = 0
    for pieces in layout:
        for dy, dz, half in pieces:
            ys = lax.rem(y + jnp.where(c == 0, 4 - dy, dy), 4)
            zs = lax.rem(z + dz + NZ, NZ)
            row = (ys // 2) * group + (zs * 2 + lax.rem(ys, 2)) * 32 + half * 16
            csc[place : place + 16, :] = cabs[pl.ds(pl.multiple_of(row, 16), 16), :]
            place += 16
    for op in wait_w:
        op.wait()
    wait_o = []
    for t in range(nsc.shape[0] // BLOCK):
        while wait_n and wait_n[0][0] < (t + 1) * BLOCK:
            wait_n.pop(0)[1].wait()
        rows = pl.ds(t * BLOCK, BLOCK)
        wait_o.append(copy(nsc.at[rows], laid.at[rows], osem.at[t]))
        block = nsc[t * BLOCK : (t + 1) * BLOCK, :]

        def mul(j):
            return jnp.dot(
                block, wsc[:, j * units : (j + 1) * units], preferred_element_type=jnp.float32
            )

        gate = mul(0)
        logistic = jax.nn.sigmoid(gate)
        curve = logistic * (1.0 - logistic) * (2.0 + gate * (1.0 - 2.0 * logistic))
        weighting = csc[t * BLOCK : (t + 1) * BLOCK, :].astype(jnp.float32) * curve * mul(1) * scale
        for p in range(2):
            second = weighting * mul(2 + p)
            out[p * units : (p + 1) * units, t * BLOCK : (t + 1) * BLOCK] = second.T.astype(
                jnp.bfloat16
            )
    for op in wait_o:
        op.wait()


def second_factor(name, layout, arrays, keep, recv, cot_keep, cot_recv, scale):
    depth = arrays[0].shape[1]
    tokens = sum(rows_of(layout))
    group, units = cot_keep.shape
    operands = (*arrays, keep, recv, cot_keep, cot_recv)
    return pl.pallas_call(
        lambda *refs: second_kernel(scale, layout, *refs),
        out_shape=(
            jax.ShapeDtypeStruct((2 * units, tokens), jnp.bfloat16),
            jax.ShapeDtypeStruct((tokens, depth), jnp.bfloat16),
        ),
        in_specs=[pl.BlockSpec(memory_space=pl.ANY)] * len(operands),
        out_specs=(pl.BlockSpec(memory_space=pltpu.VMEM), pl.BlockSpec(memory_space=pl.ANY)),
        scratch_shapes=[
            pltpu.VMEM((tokens, depth), jnp.bfloat16),
            pltpu.VMEM((depth, 4 * units), jnp.bfloat16),
            pltpu.VMEM((2 * group, units), jnp.bfloat16),
            pltpu.VMEM((tokens, units), jnp.bfloat16),
            pltpu.SemaphoreType.DMA((len(layout),)),
            pltpu.SemaphoreType.DMA((16,)),
            pltpu.SemaphoreType.DMA((2,)),
            pltpu.SemaphoreType.DMA((tokens // BLOCK,)),
        ],
        compiler_params=pltpu.CompilerParams(vmem_limit_bytes=24 * 1024 * 1024),
        cost_estimate=pl.CostEstimate(
            flops=2**20, bytes_accessed=2**20, transcendentals=0
        ),
        name=name,
    )(*operands)


def partial_kernel(tokens_e, tokens_l, second_e, second_l, own, sib):
    result = jnp.dot(second_e[...], tokens_e[...], preferred_element_type=jnp.float32)
    result = result + jnp.dot(second_l[...], tokens_l[...], preferred_element_type=jnp.float32)
    result = result.astype(jnp.bfloat16)
    step = pl.program_id(0)

    @pl.when(step == 0)
    def _():
        own[...] = result

    @pl.when(step == 1)
    def _():
        sib[...] = result


def partials(tokens_e, tokens_l, second_e, second_l, r):
    width = second_e.shape[0]
    half = jax.ShapeDtypeStruct((width, 512), jnp.bfloat16)
    whole = pl.BlockSpec((width, 512), lambda j: (0, 0))
    return pl.pallas_call(
        partial_kernel,
        grid=(2,),
        out_shape=(half, half),
        in_specs=[
            pl.BlockSpec((a.shape[0], 512), lambda j: (0, r * 2 + j)) for a in (tokens_e, tokens_l)
        ]
        + [pl.BlockSpec(a.shape, lambda j: (0, 0)) for a in (second_e, second_l)],
        out_specs=(whole, whole),
        compiler_params=pltpu.CompilerParams(vmem_limit_bytes=12 * 1024 * 1024),
        cost_estimate=pl.CostEstimate(flops=2**20, bytes_accessed=2**20, transcendentals=0),
        name="partials_%d" % r,
    )(tokens_e, tokens_l, second_e, second_l)


def final_kernel(m0, m1, m2, m3, got, out):
    units = out.shape[2] // 2
    yh = lax.axis_index("yh")
    mine = m0[...]
    for m in (m1, m2, m3):
        mine = mine + m[...].astype(jnp.float32)
    got = got[...].astype(jnp.float32)
    low, high = jnp.where(yh == 0, mine, got), jnp.where(yh == 0, got, mine)
    for p in range(2):
        rows = slice(p * units, (p + 1) * units)
        out[:, p, 0:units] = low[rows].T
        out[:, p, units : 2 * units] = high[rows].T


def finish(mine, got):
    width, rows = got.shape
    vmem = pl.BlockSpec(memory_space=pltpu.VMEM)
    return pl.pallas_call(
        final_kernel,
        out_shape=jax.ShapeDtypeStruct((rows, 2, width), jnp.float32),
        in_specs=[vmem] * 5,
        out_specs=vmem,
        compiler_params=pltpu.CompilerParams(vmem_limit_bytes=24 * 1024 * 1024),
        name="finish",
    )(*mine, got)


def lay_kernel(parts, *refs):
    outs = refs[len(refs) - len(parts) :]
    for part, out in zip(parts, outs):
        start = 0
        for i in part:
            n = refs[i].shape[0]
            out[start : start + n, :] = refs[i][...]
            start += n


def lay(name, pieces, parts):
    depth = pieces[0][0].shape[1]
    vmem = pl.BlockSpec(memory_space=pltpu.VMEM)
    return pl.pallas_call(
        lambda *refs: lay_kernel(parts, *refs),
        grid=(1,),
        out_shape=[
            jax.ShapeDtypeStruct((sum(pieces[i][2] for i in part), depth), jnp.bfloat16)
            for part in parts
        ],
        in_specs=[
            pl.BlockSpec((n, depth), lambda j, at=first // n: (at, 0)) for _, first, n in pieces
        ],
        out_specs=[
            pl.BlockSpec((sum(pieces[i][2] for i in part), depth), lambda j: (0, 0))
            for part in parts
        ],
        compiler_params=pltpu.CompilerParams(vmem_limit_bytes=12 * 1024 * 1024),
        name=name,
    )(*[a for a, _, _ in pieces])


def shift_z(v, step):
    return lax.ppermute(v, "z", [(i, (i + step) % NZ) for i in range(NZ)])


def per_device(tokens, norm_gain, w_gate, w_up, probes, cotangent):
    yh, c = lax.axis_index("yh"), lax.axis_index("c")
    units = w_gate.shape[1] // 2
    ordered = lax.optimization_barrier

    def half_of(which):
        return jnp.concatenate(
            [lax.dynamic_slice_in_dim(a, which * units, units, 1) for a in (w_gate, w_up, p0, p1)],
            axis=1,
        )

    a0, b0 = normalize(tokens, norm_gain)
    a0, b0, w_gate, w_up, probes, cotangent = ordered(
        (a0, b0, w_gate, w_up, probes, cotangent)
    )
    p0, p1 = probes[:, 0, :], probes[:, 1, :]
    w_keep, w_send = half_of(yh), half_of(1 - yh)
    keep = lax.all_gather(w_keep, ("x", "c"))

    ya = [along_y(a0, i) for i in (1, 2, 3)]
    bm, bp = shift_z(b0, 1), shift_z(b0, -1)
    *ya, bm, bp, w_send, b0 = ordered((*ya, bm, bp, w_send, b0))

    w_recv = swap_yh(w_send)
    up0, down0, y0 = lay(
        "lay_1",
        [(v, 0, 16) for v in (a0, *ya, bm, bp, b0)],
        ((0, 1, 2, 3, 4), (0, 1, 2, 3, 5), (6, 4, 5)),
    )
    up1, down1 = shift_z(up0, 1), shift_z(down0, -1)
    y1 = along_y(y0, 1)
    up1, down1, y1, w_recv, cotangent = ordered((up1, down1, y1, w_recv, cotangent))
    recv = lax.all_gather(w_recv, ("x", "c"))

    up2, down2 = shift_z(up1, 1), shift_z(down1, -1)
    cot_keep = lax.dynamic_slice_in_dim(cotangent, yh * units, units, 1)
    cot_send = lax.dynamic_slice_in_dim(cotangent, (1 - yh) * units, units, 1)
    y1, cot_send = ordered((y1, cot_send))
    (y,) = lay("lay_2", [(y1, 0, 48), (up1, 64, 16), (down1, 64, 16)], ((0, 1, 2),))
    y2 = along_y(y, 1)
    up2, down2, y2, cot_send = ordered((up2, down2, y2, cot_send))
    cot_recv = swap_yh(cot_send)

    up3, down3 = shift_z(up2, 1), shift_z(down2, -1)
    (y,) = lay("lay_3", [(y2, 0, 80), (up2, 64, 16), (down2, 64, 16)], ((0, 1, 2),))
    y3 = along_y(y, 1)
    up3, down3, y3, cot_recv, keep, recv = ordered((up3, down3, y3, cot_recv, keep, recv))

    a4 = lax.ppermute(
        jnp.where(c == 0, up3[:64], down3[:64]),
        ("c", "z"),
        ring_perm([[i * NZ + z for z in range(NZ)] for i in range(NC)], 1),
    )
    y, around, across = lay(
        "lay_4",
        [(y3, 48, 16), (y3, 64, 16), (y3, 80, 16), (y3, 96, 16)]
        + [(up3, 64, 16), (up2, 64, 16), (down2, 64, 16)],
        ((0, 1, 2, 3, 4), (5, 6, 4), (4,)),
    )
    y4, y5, y6 = along_y(y, 1), along_y(around, 3), along_y(across, 2)
    early = (up0, up1, down1, up2, down2, up3, down3, b0, bm, bp, y2, y3)
    late = (y1, y4, y5, y6, a4)

    scale = 1.0 / math.sqrt(cotangent.shape[0] * NX * NYH * NC)
    rest = (keep, recv, cot_keep, cot_recv, scale)
    second_e, tokens_e = second_factor("second_early", EARLY, early, *rest)
    second_l, tokens_l = second_factor("second_late", LATE, late, *rest)
    own, sib, first, last = {}, {}, {}, {}

    def add_cores(r):
        other = swap_core(sib[(NX - r) % NX])
        both = own[r].astype(jnp.float32) + other.astype(jnp.float32)
        pair = [lax.dynamic_slice_in_dim(both, w * 256, 256, 1) for w in (1 - yh, yh)]
        if r:
            pair = [v.astype(jnp.bfloat16) for v in pair]
        return ordered(pair[0]), ordered(pair[1])

    for r in (2, 3):
        own[r], sib[r] = partials(tokens_e, tokens_l, second_e, second_l, r)
    first[2], last[2] = add_cores(2)
    first[2], last[2], second_l = ordered((first[2], last[2], second_l))
    for r in (1, 0):
        own[r], sib[r] = partials(tokens_e, tokens_l, second_e, second_l, r)
    for r in (2, 3, 1, 0):
        if r != 2:
            first[r], last[r] = add_cores(r)
        if r:
            first[r] = along_x(first[r], NX - r)
    last[1] = along_x(last[1], NX - 1)
    *arrived, last[2], last[3] = ordered((*(first[r] for r in range(NX)), last[2], last[3]))
    total = sum(v.astype(jnp.float32) for v in arrived)
    for r in (2, 3):
        last[r] = along_x(last[r], NX - r)
    got = swap_yh(total.astype(jnp.bfloat16))
    return finish([last[r] for r in range(NX)], got)


def solution(mesh):
    inner = Mesh(mesh.devices.reshape(NX, NYH, NC, NZ, NYL), AXES)
    dp, tensor = ("x", "yh", "c"), ("z", "yl")
    in_specs = (
        P(dp + tensor, None),
        P(),
        P(dp, tensor),
        P(dp, tensor),
        P(dp, None, tensor),
        P(dp, tensor),
    )
    return jax.shard_map(
        per_device, mesh=inner, in_specs=in_specs, out_specs=P(dp, None, tensor), check_vma=False
    )
```

```python
import math

import jax
import jax.numpy as jnp
from jax import lax
from jax.experimental import pallas as pl
from jax.experimental.pallas import tpu as pltpu
from jax.sharding import Mesh, PartitionSpec as P

NX, NYH, NC, NZ, NYL = 4, 2, 2, 8, 2
AXES = ("x", "yh", "c", "z", "yl")
VMEM_BYTES = 58 * 1024 * 1024


def ring_perm(spots, step):
    size = len(spots[0])
    return [
        (line[i], line[(i + sign * step) % size])
        for line, sign in zip(spots, (1, -1))
        for i in range(size)
    ]


def along_x(v, step):
    return lax.ppermute(
        v, ("x", "c"), ring_perm([[x * 2 + c for x in range(NX)] for c in range(NC)], step)
    )


def along_y(v, step):
    spots = [[(yh * 2 + c) * 2 + yl for yh in range(NYH) for yl in range(NYL)] for c in range(NC)]
    return lax.ppermute(v, ("yh", "c", "yl"), ring_perm(spots, step))


def swap_core(v):
    return lax.ppermute(v, "c", [(0, 1), (1, 0)])


def swap_yh(v):
    return lax.ppermute(v, "yh", [(0, 1), (1, 0)])


def norm_kernel(tokens, gain, out_a, out_b):
    x, c = lax.axis_index("x"), lax.axis_index("c")
    rows, depth = tokens.shape
    piece = depth // 16
    values = tokens[...].astype(jnp.float32)
    inverse = lax.rsqrt(jnp.mean(values * values, axis=1, keepdims=True) + 1e-05)
    for r in range(NX):
        xs = lax.rem(x + jnp.where(c == 0, NX - r, r), NX)
        for yh in range(NYH):
            for crel in range(NC):
                cs = jnp.where(crel == 0, c, 1 - c)
                source = pl.multiple_of((xs * 4 + yh * 2 + cs) * piece, piece)
                block = tokens[:, pl.ds(source, piece)].astype(jnp.float32)
                normed = (block * inverse * gain[:, pl.ds(source, piece)]).astype(jnp.bfloat16)
                b = r * 4 + crel * 2 + yh
                out_a[:, b * piece : (b + 1) * piece] = normed[: rows // 2]
                out_b[:, b * piece : (b + 1) * piece] = normed[rows // 2 :]


def normalize(tokens, gain):
    rows, depth = tokens.shape
    half = jax.ShapeDtypeStruct((rows // 2, depth), jnp.bfloat16)
    return pl.pallas_call(
        norm_kernel,
        out_shape=(half, half),
        in_specs=[
            pl.BlockSpec(memory_space=pltpu.VMEM),
            pl.BlockSpec(memory_space=pltpu.VMEM),
        ],
        out_specs=(pl.BlockSpec(memory_space=pltpu.VMEM),) * 2,
        compiler_params=pltpu.CompilerParams(vmem_limit_bytes=VMEM_BYTES),
        name="rms_norm",
    )(tokens, gain.reshape(1, depth))


def _a(dz):
    return [(i, dz, 0) for i in range(4)]


EARLY = (
    _a(0),
    _a(-1) + [(0, -2, 1)],
    _a(1) + [(0, 2, 1)],
    _a(-2) + [(0, -3, 1)],
    _a(2) + [(0, 3, 1)],
    _a(-3) + [(0, 4, 1)],
    _a(3),
    [(0, 0, 1)],
    [(0, -1, 1)],
    [(0, 1, 1)],
    [(2, 0, 1), (2, -1, 1), (2, 1, 1), (1, -2, 1), (1, 2, 1)],
    [(3, 0, 1), (3, -1, 1), (3, 1, 1), (2, -2, 1), (2, 2, 1), (1, -3, 1), (1, 3, 1)],
)
LATE = (
    [(1, 0, 1), (1, -1, 1), (1, 1, 1)],
    [(3, -2, 1), (3, 2, 1), (2, -3, 1), (2, 3, 1), (1, 4, 1)],
    [(3, -3, 1), (3, 3, 1), (3, 4, 1)],
    [(2, 4, 1)],
    _a(4),
)
BLOCK = 256


def rows_of(layout):
    return [16 * len(pieces) for pieces in layout]


def second_kernel(scale, layout, *refs):
    count = len(layout)
    arrays = refs[:count]
    keep, recv, cot_keep, cot_recv, out, laid = refs[count : count + 6]
    nsc, wsc, cabs, csc, nsem, wsem, csem, osem = refs[count + 6 :]
    x, yh, c, z, yl = (lax.axis_index(a) for a in AXES)
    y = yh * 2 + yl
    group, units = cot_keep.shape

    def copy(src, dst, sem):
        op = pltpu.make_async_copy(src, dst, sem)
        op.start()
        return op

    wait_c = [
        copy(cot_keep, cabs.at[pl.ds(pl.multiple_of(yh * group, group), group)], csem.at[0]),
        copy(cot_recv, cabs.at[pl.ds(pl.multiple_of((1 - yh) * group, group), group)], csem.at[1]),
    ]
    wait_w = []
    for xs in range(NX):
        r = lax.rem(jnp.where(c == 0, x - xs, xs - x) + NX, NX)
        for cs in range(NC):
            crel = jnp.where(c == cs, 0, 1)
            for mine, bunch in ((True, keep), (False, recv)):
                row = (r * 4 + crel * 2) * 256 + jnp.where(mine, yh, 1 - yh) * 256
                wait_w.append(
                    copy(
                        bunch.at[xs * 2 + cs],
                        wsc.at[pl.ds(pl.multiple_of(row, 256), 256)],
                        wsem.at[len(wait_w)],
                    )
                )
    wait_n, start = [], 0
    for i, (array, rows) in enumerate(zip(arrays, rows_of(layout))):
        op = copy(array.at[pl.ds(0, rows)], nsc.at[pl.ds(start, rows)], nsem.at[i])
        wait_n.append((start, op))
        start += rows
    for op in wait_c:
        op.wait()
    place = 0
    for pieces in layout:
        for dy, dz, half in pieces:
            ys = lax.rem(y + jnp.where(c == 0, 4 - dy, dy), 4)
            zs = lax.rem(z + dz + NZ, NZ)
            row = (ys // 2) * group + (zs * 2 + lax.rem(ys, 2)) * 32 + half * 16
            csc[place : place + 16, :] = cabs[pl.ds(pl.multiple_of(row, 16), 16), :]
            place += 16
    for op in wait_w:
        op.wait()
    wait_o = []
    for t in range(nsc.shape[0] // BLOCK):
        while wait_n and wait_n[0][0] < (t + 1) * BLOCK:
            wait_n.pop(0)[1].wait()
        rows = pl.ds(t * BLOCK, BLOCK)
        wait_o.append(copy(nsc.at[rows], laid.at[rows], osem.at[t]))
        block = nsc[t * BLOCK : (t + 1) * BLOCK, :]

        def mul(j):
            return jnp.dot(
                block, wsc[:, j * units : (j + 1) * units], preferred_element_type=jnp.float32
            )

        gate = mul(0)
        logistic = jax.nn.sigmoid(gate)
        curve = logistic * (1.0 - logistic) * (2.0 + gate * (1.0 - 2.0 * logistic))
        weighting = csc[t * BLOCK : (t + 1) * BLOCK, :].astype(jnp.float32) * curve * mul(1) * scale
        for p in range(2):
            second = weighting * mul(2 + p)
            out[p * units : (p + 1) * units, t * BLOCK : (t + 1) * BLOCK] = second.T.astype(
                jnp.bfloat16
            )
    for op in wait_o:
        op.wait()


def second_factor(name, layout, arrays, keep, recv, cot_keep, cot_recv, scale):
    depth = arrays[0].shape[1]
    tokens = sum(rows_of(layout))
    group, units = cot_keep.shape
    operands = (*arrays, keep, recv, cot_keep, cot_recv)
    return pl.pallas_call(
        lambda *refs: second_kernel(scale, layout, *refs),
        out_shape=(
            jax.ShapeDtypeStruct((2 * units, tokens), jnp.bfloat16),
            jax.ShapeDtypeStruct((tokens, depth), jnp.bfloat16),
        ),
        in_specs=[pl.BlockSpec(memory_space=pl.ANY)] * len(operands),
        out_specs=(pl.BlockSpec(memory_space=pltpu.VMEM), pl.BlockSpec(memory_space=pl.ANY)),
        scratch_shapes=[
            pltpu.VMEM((tokens, depth), jnp.bfloat16),
            pltpu.VMEM((depth, 4 * units), jnp.bfloat16),
            pltpu.VMEM((2 * group, units), jnp.bfloat16),
            pltpu.VMEM((tokens, units), jnp.bfloat16),
            pltpu.SemaphoreType.DMA((len(layout),)),
            pltpu.SemaphoreType.DMA((16,)),
            pltpu.SemaphoreType.DMA((2,)),
            pltpu.SemaphoreType.DMA((tokens // BLOCK,)),
        ],
        compiler_params=pltpu.CompilerParams(vmem_limit_bytes=24 * 1024 * 1024),
        cost_estimate=pl.CostEstimate(
            flops=2**20, bytes_accessed=2**20, transcendentals=0
        ),
        name=name,
    )(*operands)


def partial_kernel(tokens_e, tokens_l, second_e, second_l, own, sib):
    result = jnp.dot(second_e[...], tokens_e[...], preferred_element_type=jnp.float32)
    result = result + jnp.dot(second_l[...], tokens_l[...], preferred_element_type=jnp.float32)
    result = result.astype(jnp.bfloat16)
    step = pl.program_id(0)

    @pl.when(step == 0)
    def _():
        own[...] = result

    @pl.when(step == 1)
    def _():
        sib[...] = result


def partials(tokens_e, tokens_l, second_e, second_l, r):
    width = second_e.shape[0]
    half = jax.ShapeDtypeStruct((width, 512), jnp.bfloat16)
    whole = pl.BlockSpec((width, 512), lambda j: (0, 0))
    return pl.pallas_call(
        partial_kernel,
        grid=(2,),
        out_shape=(half, half),
        in_specs=[
            pl.BlockSpec((a.shape[0], 512), lambda j: (0, r * 2 + j)) for a in (tokens_e, tokens_l)
        ]
        + [pl.BlockSpec(a.shape, lambda j: (0, 0)) for a in (second_e, second_l)],
        out_specs=(whole, whole),
        compiler_params=pltpu.CompilerParams(vmem_limit_bytes=12 * 1024 * 1024),
        cost_estimate=pl.CostEstimate(flops=2**20, bytes_accessed=2**20, transcendentals=0),
        name="partials_%d" % r,
    )(tokens_e, tokens_l, second_e, second_l)


def final_kernel(m0, m1, m2, m3, got, out):
    units = out.shape[2] // 2
    yh = lax.axis_index("yh")
    mine = m0[...]
    for m in (m1, m2, m3):
        mine = mine + m[...].astype(jnp.float32)
    got = got[...].astype(jnp.float32)
    low, high = jnp.where(yh == 0, mine, got), jnp.where(yh == 0, got, mine)
    for p in range(2):
        rows = slice(p * units, (p + 1) * units)
        out[:, p, 0:units] = low[rows].T
        out[:, p, units : 2 * units] = high[rows].T


def finish(mine, got):
    width, rows = got.shape
    vmem = pl.BlockSpec(memory_space=pltpu.VMEM)
    return pl.pallas_call(
        final_kernel,
        out_shape=jax.ShapeDtypeStruct((rows, 2, width), jnp.float32),
        in_specs=[vmem] * 5,
        out_specs=vmem,
        compiler_params=pltpu.CompilerParams(vmem_limit_bytes=24 * 1024 * 1024),
        name="finish",
    )(*mine, got)


def lay_kernel(parts, *refs):
    outs = refs[len(refs) - len(parts) :]
    for part, out in zip(parts, outs):
        start = 0
        for i in part:
            n = refs[i].shape[0]
            out[start : start + n, :] = refs[i][...]
            start += n


def lay(name, pieces, parts):
    depth = pieces[0][0].shape[1]
    vmem = pl.BlockSpec(memory_space=pltpu.VMEM)
    return pl.pallas_call(
        lambda *refs: lay_kernel(parts, *refs),
        grid=(1,),
        out_shape=[
            jax.ShapeDtypeStruct((sum(pieces[i][2] for i in part), depth), jnp.bfloat16)
            for part in parts
        ],
        in_specs=[
            pl.BlockSpec((n, depth), lambda j, at=first // n: (at, 0)) for _, first, n in pieces
        ],
        out_specs=[
            pl.BlockSpec((sum(pieces[i][2] for i in part), depth), lambda j: (0, 0))
            for part in parts
        ],
        compiler_params=pltpu.CompilerParams(vmem_limit_bytes=12 * 1024 * 1024),
        name=name,
    )(*[a for a, _, _ in pieces])


def shift_z(v, step):
    return lax.ppermute(v, "z", [(i, (i + step) % NZ) for i in range(NZ)])


def per_device(tokens, norm_gain, w_gate, w_up, probes, cotangent):
    yh, c = lax.axis_index("yh"), lax.axis_index("c")
    units = w_gate.shape[1] // 2
    ordered = lax.optimization_barrier

    def half_of(which):
        return jnp.concatenate(
            [lax.dynamic_slice_in_dim(a, which * units, units, 1) for a in (w_gate, w_up, p0, p1)],
            axis=1,
        )

    a0, b0 = normalize(tokens, norm_gain)
    a0, b0, w_gate, w_up, probes, cotangent = ordered(
        (a0, b0, w_gate, w_up, probes, cotangent)
    )
    p0, p1 = probes[:, 0, :], probes[:, 1, :]
    w_keep, w_send = half_of(yh), half_of(1 - yh)
    keep = lax.all_gather(w_keep, ("x", "c"))

    ya = [along_y(a0, i) for i in (1, 2, 3)]
    bm, bp = shift_z(b0, 1), shift_z(b0, -1)
    *ya, bm, bp, w_send, b0 = ordered((*ya, bm, bp, w_send, b0))

    w_recv = swap_yh(w_send)
    up0, down0, y0 = lay(
        "lay_1",
        [(v, 0, 16) for v in (a0, *ya, bm, bp, b0)],
        ((0, 1, 2, 3, 4), (0, 1, 2, 3, 5), (6, 4, 5)),
    )
    up1, down1 = shift_z(up0, 1), shift_z(down0, -1)
    y1 = along_y(y0, 1)
    up1, down1, y1, w_recv, cotangent = ordered((up1, down1, y1, w_recv, cotangent))
    recv = lax.all_gather(w_recv, ("x", "c"))

    up2, down2 = shift_z(up1, 1), shift_z(down1, -1)
    cot_keep = lax.dynamic_slice_in_dim(cotangent, yh * units, units, 1)
    cot_send = lax.dynamic_slice_in_dim(cotangent, (1 - yh) * units, units, 1)
    y1, cot_send = ordered((y1, cot_send))
    (y,) = lay("lay_2", [(y1, 0, 48), (up1, 64, 16), (down1, 64, 16)], ((0, 1, 2),))
    y2 = along_y(y, 1)
    up2, down2, y2, cot_send = ordered((up2, down2, y2, cot_send))
    cot_recv = swap_yh(cot_send)

    y, down = lay(
        "lay_3",
        [(y2, 0, 80), (up2, 64, 16), (down2, 64, 16), (down2, 0, 64)],
        ((0, 1, 2), (3,)),
    )
    up3, down3 = shift_z(up2, 1), shift_z(down, -1)
    y3 = along_y(y, 1)
    up3, down3, y3, cot_recv, keep, recv = ordered((up3, down3, y3, cot_recv, keep, recv))

    a4 = lax.ppermute(
        jnp.where(c == 0, up3[:64], down3),
        ("c", "z"),
        ring_perm([[i * NZ + z for z in range(NZ)] for i in range(NC)], 1),
    )
    y, around, across = lay(
        "lay_4",
        [(y3, 48, 16), (y3, 64, 16), (y3, 80, 16), (y3, 96, 16)]
        + [(up3, 64, 16), (up2, 64, 16), (down2, 64, 16)],
        ((0, 1, 2, 3, 4), (5, 6, 4), (4,)),
    )
    y4, y5, y6 = along_y(y, 1), along_y(around, 3), along_y(across, 2)
    early = (up0, up1, down1, up2, down2, up3, down3, b0, bm, bp, y2, y3)
    late = (y1, y4, y5, y6, a4)

    scale = 1.0 / math.sqrt(cotangent.shape[0] * NX * NYH * NC)
    rest = (keep, recv, cot_keep, cot_recv, scale)
    second_e, tokens_e = second_factor("second_early", EARLY, early, *rest)
    second_l, tokens_l = second_factor("second_late", LATE, late, *rest)
    own, sib, first, last = {}, {}, {}, {}

    def add_cores(r):
        other = swap_core(sib[(NX - r) % NX])
        both = own[r].astype(jnp.float32) + other.astype(jnp.float32)
        pair = [lax.dynamic_slice_in_dim(both, w * 256, 256, 1) for w in (1 - yh, yh)]
        if r:
            pair = [v.astype(jnp.bfloat16) for v in pair]
        return ordered(pair[0]), ordered(pair[1])

    for r in (2, 3):
        own[r], sib[r] = partials(tokens_e, tokens_l, second_e, second_l, r)
    first[2], last[2] = add_cores(2)
    first[2], last[2], second_l = ordered((first[2], last[2], second_l))
    for r in (1, 0):
        own[r], sib[r] = partials(tokens_e, tokens_l, second_e, second_l, r)
    for r in (2, 3, 1, 0):
        if r != 2:
            first[r], last[r] = add_cores(r)
        if r:
            first[r] = along_x(first[r], NX - r)
    last[1] = along_x(last[1], NX - 1)
    *arrived, last[2], last[3] = ordered((*(first[r] for r in range(NX)), last[2], last[3]))
    total = sum(v.astype(jnp.float32) for v in arrived)
    for r in (2, 3):
        last[r] = along_x(last[r], NX - r)
    got = swap_yh(total.astype(jnp.bfloat16))
    return finish([last[r] for r in range(NX)], got)


def solution(mesh):
    inner = Mesh(mesh.devices.reshape(NX, NYH, NC, NZ, NYL), AXES)
    dp, tensor = ("x", "yh", "c"), ("z", "yl")
    in_specs = (
        P(dp + tensor, None),
        P(),
        P(dp, tensor),
        P(dp, tensor),
        P(dp, None, tensor),
        P(dp, tensor),
    )
    return jax.shard_map(
        per_device, mesh=inner, in_specs=in_specs, out_specs=P(dp, None, tensor), check_vma=False
    )
```
